128 devices in a mesh: month: 4 (over x_hi, core), mascon: 32 (over z, y, x_lo).
Axes of the slice: x: 4 (x_hi: 2, x_lo: 2; x = x_hi * 2 + x_lo), y: 4, z: 4, core: 2. Of those that a mesh axis runs over, the one named last changes fastest.
Arguments:
- panels: bfloat16 [32, 128, 40960], P('month', None, 'mascon'), may hold values from -0.0546875 to 0.0546875
- observations: bfloat16 [32, 128, 256], P('month'), may hold values from -6 to 6
- data_weights: bfloat16 [32, 128], P('month'), may hold values from 0.25 to 2
- arc_month: int32 [32], replicated, may hold values from 0 to 3, as said below
- fields: float32 [4, 40960, 256], P('month', 'mascon'), may hold values from -6 to 6
- diag_scale: float32 [4, 40960], P('month', 'mascon'), may hold values from 1.5 to 6
- smooth_coef: float32 [6, 40960], P(None, 'mascon'), may hold values from 0.05 to 0.5
- neighbours: int32 [6, 40960], P(None, 'mascon'), may hold values from 0 to 40959, as said below
- time_coupling: float32 [40960], P('mascon'), may hold values from 0.1 to 1
Outputs:
- solution: float32 [4, 40960, 256], P('month', 'mascon')
The draws below stay inside these ranges and needn't reach their ends.
Inputs may be any that keep to these rules, and one draw needn't show every extreme that they name: `arc_month`: within each aligned block of 8 arcs, at most 4 arcs have months in any one group of 1 consecutive months (months g * 1 to (g + 1) - 1); one such group receives exactly 4 arcs from every block. `neighbours`: each stencil neighbour lies within 64 positions of its mascon in the cyclic mascon order, and is never the mascon itself.
All inputs are finite; a program needn't handle non-finite values.
Results may differ from the reference program's by a relative error of at most 0.0009.
Values may be sent and summed in bfloat16 or wider, within the bound.
A program may use at most 128 MiB of HBM per device.

```python
import math
import jax
import jax.numpy as jnp
from jax import lax

MASCONS = 40960
SAMPLES = 256
ARC_ROWS = 128
A_DEV = 8
CAP = 4
ARCS = 32
MON_DEV = 1
MONTHS = 4
NB = 6
HALO = 64
ITERS = 2


def draw_arc_month(key, part):
    key = jax.random.fold_in(key, 7)
    key_one, key_two, key_three, key_four = jax.random.split(key, 4)
    groups = MONTHS // MON_DEV
    blocks = ARCS // A_DEV
    heavy = jax.random.randint(key_one, (), 0, groups)
    others = (heavy + jax.random.randint(key_two, (blocks, A_DEV - CAP), 1, groups)) % groups
    group_of = jnp.concatenate([jnp.full((blocks, CAP), heavy, jnp.int32), others.astype(jnp.int32)], axis=1)
    month = group_of * MON_DEV + jax.random.randint(key_three, (blocks, A_DEV), 0, MON_DEV)
    row_keys = jax.random.split(key_four, blocks)
    month = jax.vmap(lambda row_key, row: jax.random.permutation(row_key, row))(row_keys, month)
    return month.reshape(ARCS).astype(jnp.int32)


def draw_neighbours(key, part):
    key = jax.random.fold_in(key, 13)
    key_one, key_two = jax.random.split(key, 2)
    reach = jax.random.randint(key_one, (NB, MASCONS), 1, HALO + 1)
    signs = jax.random.randint(key_two, (NB, MASCONS), 0, 2) * 2 - 1
    places = jnp.arange(MASCONS, dtype=jnp.int32)[None, :]
    return ((places + signs * reach) % MASCONS).astype(jnp.int32)


def shard_levels(rng, extent, shards, smallest, top_value):
    def one(position, blocks):
        heights = jax.random.uniform(jax.random.fold_in(jax.random.fold_in(rng, 6), position), (blocks,), jnp.float32, smallest / len(shards), top_value / len(shards))
        return jnp.repeat(jnp.exp(heights), extent[position] // blocks).reshape((-1,) + (1,) * (len(extent) - position - 1))

    level = one(*shards[0])
    for cut in shards[1:]:
        level = level * one(*cut)
    return level


def bell_draw(own_key, dims, spread, most, shards=(), held_as=jnp.bfloat16):
    drawn = spread * jax.random.normal(own_key, dims, jnp.float32)
    if shards:
        drawn = drawn * shard_levels(own_key, dims, shards, -0.22, 0.18)
    return jnp.clip(drawn, -most, most).astype(held_as)


def setup_inputs(seed: int = 0) -> dict:
    seeds = jax.random.split(jax.random.key(seed), 10)
    panels = bell_draw(seeds[0], (ARCS, ARC_ROWS, MASCONS), (2 * (MASCONS * A_DEV * ARC_ROWS // MON_DEV) ** 0.5) ** -0.5, 0.0546875, ((0, 4), (2, 32)))
    observations = bell_draw(seeds[1], (ARCS, ARC_ROWS, SAMPLES), 1.0, 6.0, ((0, 4),))
    data_weights = jnp.clip(jnp.exp(math.log(2.0) - 2.0794415 * jax.random.uniform(seeds[2], (ARCS, ARC_ROWS), jnp.float32) ** shard_levels(seeds[2], (ARCS, ARC_ROWS), ((0, 4),), -0.2, 0.2)), 0.25, 2.0).astype(jnp.bfloat16)
    arc_month = draw_arc_month(jax.random.fold_in(seeds[9], 71), 0)
    fields = bell_draw(seeds[4], (MONTHS, MASCONS, SAMPLES), 1.0, 6.0, ((0, 4), (1, 32)), jnp.float32)
    diag_scale = jnp.clip(jnp.exp(math.log(6.0) - 1.3862944 * jax.random.uniform(seeds[5], (MONTHS, MASCONS), jnp.float32) ** shard_levels(seeds[5], (MONTHS, MASCONS), ((0, 4), (1, 32)), -0.2, 0.2)), 1.5, 6.0)
    smooth_coef = jnp.clip(jnp.exp(math.log(0.5) - 2.3025851 * jax.random.uniform(seeds[6], (NB, MASCONS), jnp.float32) ** shard_levels(seeds[6], (NB, MASCONS), ((1, 32),), -0.2, 0.2)), 0.05, 0.5)
    neighbours = draw_neighbours(jax.random.fold_in(seeds[9], 71), 0)
    time_coupling = jnp.clip(jnp.exp(math.log(1.0) - 2.3025851 * jax.random.uniform(seeds[8], (MASCONS,), jnp.float32) ** shard_levels(seeds[8], (MASCONS,), ((0, 32),), -0.2, 0.2)), 0.1, 1.0)
    return dict(panels=panels, observations=observations, data_weights=data_weights, arc_month=arc_month, fields=fields, diag_scale=diag_scale, smooth_coef=smooth_coef, neighbours=neighbours, time_coupling=time_coupling)


relax_factor = 0.5


def smooth(state, smooth_coef, neighbours, time_coupling):
    lap_term = jnp.zeros_like(state)
    for which in range(NB):
        lap_term = lap_term + smooth_coef[which][None, :, None] * (state - jnp.take(state, neighbours[which], axis=1))
    padded = jnp.pad(state, ((1, 1), (0, 0), (0, 0)))
    return lap_term + time_coupling[None, :, None] * (2.0 * state - padded[:-2] - padded[2:])


def reference(panels, observations, data_weights, arc_month, fields, diag_scale, smooth_coef, neighbours, time_coupling):
    state = fields
    for step in range(ITERS):
        state_bf = state.astype(jnp.bfloat16)

        def arc_step(gradient, item):
            panel, obs_rows, weight_rows, month = item
            chosen = lax.dynamic_index_in_dim(state_bf, month, 0, keepdims=False)
            track = jnp.dot(panel, chosen, preferred_element_type=jnp.float32)
            weighted = (weight_rows.astype(jnp.float32)[:, None] * (track - obs_rows.astype(jnp.float32))).astype(jnp.bfloat16)
            term = jnp.dot(panel.T, weighted, preferred_element_type=jnp.float32)
            current = lax.dynamic_index_in_dim(gradient, month, 0, keepdims=False)
            return lax.dynamic_update_index_in_dim(gradient, current + term, month, 0), None

        gradient = jnp.zeros(state.shape, jnp.float32)
        gradient, unused = lax.scan(arc_step, gradient, (panels, observations, data_weights, arc_month.astype(jnp.int32)))
        smoothing = smooth(state, smooth_coef, neighbours, time_coupling)
        state = state - relax_factor * (gradient + smoothing) / diag_scale[:, :, None]
    return state
```

```python
import functools

import jax
import jax.numpy as jnp
from jax import lax
from jax.experimental import pallas as pl
from jax.experimental.pallas import tpu as pltpu
from jax.sharding import PartitionSpec as P

MESH = pl.DeviceIdType.MESH
HALO = 64
ITERS = 2
HALVES = 2
BLOCK = 128
LEVELS = 32767.0
RELAX = 0.5

F32, BF16, I16 = jnp.float32, jnp.bfloat16, jnp.int16


def encode(x):
    top = jnp.maximum(jnp.max(jnp.abs(x), axis=0, keepdims=True), 1e-30)
    code = jnp.round(x * (LEVELS / top)).astype(jnp.int32).astype(I16)
    return code, top * (1.0 / LEVELS)


def decode(code, scale):
    return code.astype(jnp.int32).astype(F32) * scale


def kernel(
    shape,
    arc_month,
    panels_hbm,
    obs,
    weights,
    fields,
    diag,
    coef,
    neighbours,
    coupling,
    out,
    panels,
    turned,
    wide,
    coded,
    scales,
    states,
    track,
    partial,
    lane_sum,
    lane_got,
    resid,
    masked,
    grad_own,
    grad_code,
    grad_scale,
    grad_code_in,
    grad_scale_in,
    base,
    weight_rows,
    stencil,
    keep_rows,
    step_rows,
    time_rows,
    columns,
    split,
    load_sem,
    plane_send,
    plane_recv,
    one_send,
    one_recv,
    turn_sem,
):
    cols, arcs, rows, total = shape
    blocks = cols // BLOCK
    piece = arcs * rows // 16
    g, s = lax.axis_index("month"), lax.axis_index("mascon")
    core, hi = g % 2, g // 2
    z, y, x_lo = s // 8, (s // 2) % 4, s % 2
    q = z * 4 + y
    mate_month = g + 1 - 2 * core
    pair_month = (g + 2) % 4
    mate = (mate_month, s)
    pair = (pair_month, s)
    beside = (g, s + 1 - 2 * x_lo)
    right = (g, (s + 1) % 32)
    left = (g, (s + 31) % 32)

    def peer(d):
        return ((z + d // 4) % 4) * 4 + (y + d % 4) % 4

    def device(p):
        return (g, p * 2 + x_lo)

    load = pltpu.make_async_copy(panels_hbm, panels, load_sem)
    load.start()

    barrier = pltpu.get_barrier_semaphore()

    def greet(d, carry):
        pl.semaphore_signal(barrier, inc=1, device_id=device(peer(d)), device_id_type=MESH)
        return carry

    lax.fori_loop(1, 16, greet, 0)
    for other in (mate, pair, left, right):
        pl.semaphore_signal(barrier, inc=1, device_id=other, device_id_type=MESH)
    pl.semaphore_wait(barrier, 19)

    names = ("pc", "ps", "mc", "ms", "fc", "fs", "hl", "hr", "xl", "wm", "gc", "gs")

    targets = dict(zip(names, (pair, pair, mate, mate, mate, mate, left, right, beside, mate, pair, pair)))

    def plane(it, h, phase, d, src, dst):
        return pltpu.make_async_remote_copy(
            src_ref=src,
            dst_ref=dst,
            send_sem=plane_send.at[(it * HALVES + h) * 2 + phase, d],
            recv_sem=plane_recv.at[(it * HALVES + h) * 2 + phase, d],
            device_id=device(peer(d)),
            device_id_type=MESH,
        )

    def copy(it, h, name):
        w = wide.at[it, h]
        mine, theirs = (it, h, g), (it, h, pair_month)
        after, before = pl.ds(HALO + cols, HALO), pl.ds(0, HALO)
        if name in ("pc", "mc"):
            src, dst = coded.at[mine], coded.at[mine]
        elif name in ("ps", "ms"):
            src, dst = scales.at[mine], scales.at[mine]
        elif name == "fc":
            src, dst = coded.at[theirs], coded.at[theirs]
        elif name == "fs":
            src, dst = scales.at[theirs], scales.at[theirs]
        elif name == "hl":
            src, dst = w.at[pl.ds(HALO, HALO)], w.at[after]
        elif name == "hr":
            src, dst = w.at[pl.ds(cols, HALO)], w.at[before]
        elif name == "xl":
            src, dst = lane_sum.at[it, h], lane_got.at[it, h]
        elif name == "wm":
            src, dst = resid.at[it, h, core], resid.at[it, h, core]
        elif name == "gc":
            src, dst = grad_code.at[it, h], grad_code_in.at[it, h]
        else:
            src, dst = grad_scale.at[it, h], grad_scale_in.at[it, h]
        i = names.index(name)
        return pltpu.make_async_remote_copy(
            src_ref=src,
            dst_ref=dst,
            send_sem=one_send.at[it * HALVES + h, i],
            recv_sem=one_recv.at[it * HALVES + h, i],
            device_id=targets[name],
            device_id_type=MESH,
        )

    def reduce_copy(it, h, d):
        start = pl.multiple_of(peer(d) * piece, piece)
        return plane(it, h, 0, d, track.at[it, h, pl.ds(start, piece)], partial.at[it, h, d])

    def gather_copy(it, h, d):
        start = pl.multiple_of(q * piece, piece)
        own = resid.at[it, h, core, pl.ds(start, piece)]
        return plane(it, h, 1, d, own, own)

    def over_blocks(body):
        def run(b, carry):
            body(b, pl.multiple_of(b * BLOCK, BLOCK))
            return carry

        lax.fori_loop(0, blocks, run, 0)

    def offer(it, h):
        if it == 0:
            wide[it, h, pl.ds(HALO, cols), :] = fields[0, :, pl.ds(h * BLOCK, BLOCK)]
        copy(it, h, "hl").start()
        copy(it, h, "hr").start()

        def body(b, r):
            x = wide[it, h, pl.ds(HALO + r, BLOCK), :]
            code, scale = encode(x)
            coded[it, h, g, pl.ds(r, BLOCK), :] = code
            scales[it, h, g, pl.ds(b, 1), :] = scale
            states[h, g, pl.ds(r, BLOCK), :] = x.astype(BF16)

        over_blocks(body)
        for name in ("pc", "ps", "mc", "ms"):
            copy(it, h, name).start()

    def unpack(it, h, month):
        def body(b, r):
            x = decode(coded[it, h, month, pl.ds(r, BLOCK), :], scales[it, h, month, pl.ds(b, 1), :])
            states[h, month, pl.ds(r, BLOCK), :] = x.astype(BF16)

        over_blocks(body)

    def gather_months(it, h):
        copy(it, h, "mc").wait_recv()
        copy(it, h, "ms").wait_recv()
        unpack(it, h, mate_month)
        copy(it, h, "pc").wait_recv()
        copy(it, h, "ps").wait_recv()
        copy(it, h, "fc").start()
        copy(it, h, "fs").start()
        unpack(it, h, pair_month)
        copy(it, h, "fc").wait_recv()
        copy(it, h, "fs").wait_recv()
        unpack(it, h, (mate_month + 2) % 4)

    def predict(it, h):
        def arc(a, carry):
            month = arc_month[g * arcs + a]
            track[it, h, pl.ds(pl.multiple_of(a * rows, rows), rows), :] = jnp.dot(
                panels[a], states[h, month], preferred_element_type=F32
            )
            return carry

        lax.fori_loop(0, arcs, arc, 0)

        def go(d, carry):
            reduce_copy(it, h, d).start()
            return carry

        lax.fori_loop(1, 16, go, 0)

    def reduce_plane(it, h):
        start = pl.multiple_of(q * piece, piece)

        def add(d, acc):
            reduce_copy(it, h, d).wait_recv()
            return acc + partial[it, h, d]

        lane_sum[it, h] = lax.fori_loop(1, 16, add, track[it, h, pl.ds(start, piece), :])
        copy(it, h, "xl").start()

    def weigh(it, h):
        start = pl.multiple_of(q * piece, piece)
        copy(it, h, "xl").wait_recv()
        full = lane_sum[it, h] + lane_got[it, h]
        seen = obs[pl.ds(start, piece), pl.ds(h * BLOCK, BLOCK)].astype(F32)
        resid[it, h, core, pl.ds(start, piece), :] = (weight_rows[pl.ds(start, piece), :] * (full - seen)).astype(BF16)

        def go(d, carry):
            gather_copy(it, h, d).start()
            return carry

        lax.fori_loop(1, 16, go, 0)

    def gather_resid(it, h):
        def got(d, carry):
            gather_copy(it, h, d).wait_recv()
            return carry

        lax.fori_loop(1, 16, got, 0)
        copy(it, h, "wm").start()

    def gradients(it, h):

        def place(blk):
            def arc(a, carry):
                month = arc_month[(hi * 2 + blk) * arcs + a]
                r = pl.multiple_of(a * rows, rows)
                w = resid[it, h, blk, pl.ds(r, rows), :].astype(F32)
                masked[blk, pl.ds(r, rows), pl.ds(0, BLOCK)] = jnp.where(month == pair_month, w, 0.0).astype(BF16)
                masked[blk, pl.ds(r, rows), pl.ds(BLOCK, BLOCK)] = jnp.where(month == g, w, 0.0).astype(BF16)
                return carry

            lax.fori_loop(0, arcs, arc, 0)

        place(core)
        copy(it, h, "wm").wait_recv()
        place(1 - core)

        def body(b, r):
            both = jnp.dot(turned[0, pl.ds(r, BLOCK), :], masked[0], preferred_element_type=F32) + jnp.dot(
                turned[1, pl.ds(r, BLOCK), :], masked[1], preferred_element_type=F32
            )
            code, scale = encode(both[:, :BLOCK])
            grad_code[it, h, pl.ds(r, BLOCK), :] = code
            grad_scale[it, h, pl.ds(b, 1), :] = scale
            grad_own[h, pl.ds(r, BLOCK), :] = both[:, BLOCK:]

        over_blocks(body)
        copy(it, h, "gc").start()
        copy(it, h, "gs").start()

    def smooth(it, h):
        copy(it, h, "hl").wait_recv()
        copy(it, h, "hr").wait_recv()
        first = jnp.where(g == 0, 0.0, 1.0)
        last = jnp.where(g == 3, 0.0, 1.0)
        before, after = jnp.maximum(g - 1, 0), jnp.minimum(g + 1, 3)
        w = wide[it, h]
        high = w.astype(BF16)
        split[0] = high
        split[1] = (w - high.astype(F32)).astype(BF16)

        def body(b, r):
            window = jnp.concatenate(
                [split[0, pl.ds(r, 2 * BLOCK), :], split[0, pl.ds(r, 2 * BLOCK), :], split[1, pl.ds(r, 2 * BLOCK), :]],
                axis=0,
            )
            near = jnp.dot(stencil[b], window, preferred_element_type=F32)
            old = first * decode(coded[it, h, before, pl.ds(r, BLOCK), :], scales[it, h, before, pl.ds(b, 1), :])
            new = last * decode(coded[it, h, after, pl.ds(r, BLOCK), :], scales[it, h, after, pl.ds(b, 1), :])
            base[h, pl.ds(r, BLOCK), :] = (
                wide[it, h, pl.ds(HALO + r, BLOCK), :] * keep_rows[pl.ds(r, BLOCK), :]
                + near
                + time_rows[pl.ds(r, BLOCK), :] * (old + new)
            )

        over_blocks(body)

    def update(it, h):
        copy(it, h, "gc").wait_recv()
        copy(it, h, "gs").wait_recv()

        def body(b, r):
            theirs = decode(grad_code_in[it, h, pl.ds(r, BLOCK), :], grad_scale_in[it, h, pl.ds(b, 1), :])
            new = base[h, pl.ds(r, BLOCK), :] - step_rows[pl.ds(r, BLOCK), :] * (
                grad_own[h, pl.ds(r, BLOCK), :] + theirs
            )
            if it == ITERS - 1:
                out[0, pl.ds(r, BLOCK), pl.ds(h * BLOCK, BLOCK)] = new
            else:
                wide[it + 1, h, pl.ds(HALO + r, BLOCK), :] = new

        over_blocks(body)

    turn = pltpu.make_async_remote_copy(
        src_ref=turned.at[core],
        dst_ref=turned.at[core],
        send_sem=turn_sem.at[0],
        recv_sem=turn_sem.at[1],
        device_id=mate,
        device_id_type=MESH,
    )

    def prepare():
        load.wait()

        def arc(a, carry):
            turned[core, :, pl.ds(pl.multiple_of(a * rows, rows), rows)] = panels[a].T
            return carry

        lax.fori_loop(0, arcs, arc, 0)
        turn.start()

        by_row = weights[...].astype(F32).T
        for a in range(arcs):
            weight_rows[a * rows : (a + 1) * rows, :] = jnp.broadcast_to(by_row[:, a : a + 1], (rows, BLOCK))

        count = neighbours.shape[0]
        here = s * cols + lax.broadcasted_iota(jnp.int32, (count, cols), 1)
        offset = neighbours[...] - here + HALO
        offset = jnp.where(offset < 0, offset + total, offset)
        offset = jnp.where(offset >= total, offset - total, offset)
        step = RELAX / diag[...]
        near = coef[...]
        own = jnp.sum(near, axis=0, keepdims=True)
        table = jnp.concatenate(
            [
                offset.astype(F32),
                near * step,
                step,
                1.0 - step * (own + 2.0 * coupling[...]),
                step * coupling[...],
                jnp.zeros_like(step),
            ],
            axis=0,
        )
        columns[...] = table.T

        def body(b, r):
            part = columns[pl.ds(r, BLOCK), :]
            place = (
                lax.broadcasted_iota(jnp.int32, (BLOCK, 2 * BLOCK), 1)
                - lax.broadcasted_iota(jnp.int32, (BLOCK, 2 * BLOCK), 0)
            ).astype(F32)
            band = jnp.zeros((BLOCK, 2 * BLOCK), F32)
            for n in range(count):
                band = band + jnp.where(place == part[:, n : n + 1], part[:, count + n : count + n + 1], 0.0)
            high = band.astype(BF16)
            low = (band - high.astype(F32)).astype(BF16)
            stencil[b, :, pl.ds(0, 2 * BLOCK)] = high
            stencil[b, :, pl.ds(2 * BLOCK, 2 * BLOCK)] = low
            stencil[b, :, pl.ds(4 * BLOCK, 2 * BLOCK)] = high
            for k, where in enumerate((step_rows, keep_rows, time_rows)):
                where[pl.ds(r, BLOCK), :] = jnp.broadcast_to(
                    part[:, 2 * count + k : 2 * count + k + 1], (BLOCK, BLOCK)
                )

        over_blocks(body)

    offer(0, 0)
    offer(0, 1)
    prepare()
    for it in range(ITERS):
        for h in range(HALVES):
            gather_months(it, h)
            predict(it, h)
        smooth(it, 0)
        for h in range(HALVES):
            reduce_plane(it, h)
        for h in range(HALVES):
            weigh(it, h)
        smooth(it, 1)
        for h in range(HALVES):
            gather_resid(it, h)
        if it == 0:
            turn.wait()
        for h in range(HALVES):
            gradients(it, h)
        for h in range(HALVES):
            update(it, h)
            if it + 1 < ITERS:
                offer(it + 1, h)

    for it in range(ITERS):
        for h in range(HALVES):
            for name in names:
                copy(it, h, name).wait_send()

            def sent(d, carry):
                reduce_copy(it, h, d).wait_send()
                gather_copy(it, h, d).wait_send()
                return carry

            lax.fori_loop(1, 16, sent, 0)


def on_device(panels, observations, data_weights, arc_month, fields, diag_scale, smooth_coef, neighbours, time_coupling):
    arcs, rows, cols = panels.shape
    samples = fields.shape[2]
    total = cols * lax.axis_size("mascon")
    every = arcs * rows
    piece = every // 16
    stages = (ITERS, HALVES)
    vmem = pl.BlockSpec(memory_space=pltpu.VMEM)
    return pl.pallas_call(
        functools.partial(kernel, (cols, arcs, rows, total)),
        out_shape=jax.ShapeDtypeStruct(fields.shape, F32),
        in_specs=[pl.BlockSpec(memory_space=pltpu.SMEM), pl.BlockSpec(memory_space=pl.ANY)] + [vmem] * 7,
        out_specs=vmem,
        scratch_shapes=[
            pltpu.VMEM(panels.shape, BF16),
            pltpu.VMEM((2, cols, every), BF16),
            pltpu.VMEM(stages + (cols + 2 * HALO, BLOCK), F32),
            pltpu.VMEM(stages + (4, cols, BLOCK), I16),
            pltpu.VMEM(stages + (4, 16, BLOCK), F32),
            pltpu.VMEM((HALVES, 4, cols, BLOCK), BF16),
            pltpu.VMEM(stages + (every, BLOCK), F32),
            pltpu.VMEM(stages + (16, piece, BLOCK), F32),
            pltpu.VMEM(stages + (piece, BLOCK), F32),
            pltpu.VMEM(stages + (piece, BLOCK), F32),
            pltpu.VMEM(stages + (2, every, BLOCK), BF16),
            pltpu.VMEM((2, every, 2 * BLOCK), BF16),
            pltpu.VMEM((HALVES, cols, BLOCK), F32),
            pltpu.VMEM(stages + (cols, BLOCK), I16),
            pltpu.VMEM(stages + (16, BLOCK), F32),
            pltpu.VMEM(stages + (cols, BLOCK), I16),
            pltpu.VMEM(stages + (16, BLOCK), F32),
            pltpu.VMEM((HALVES, cols, BLOCK), F32),
            pltpu.VMEM((every, BLOCK), F32),
            pltpu.VMEM((cols // BLOCK, BLOCK, 6 * BLOCK), BF16),
            pltpu.VMEM((cols, BLOCK), F32),
            pltpu.VMEM((cols, BLOCK), F32),
            pltpu.VMEM((cols, BLOCK), F32),
            pltpu.VMEM((cols, 16), F32),
            pltpu.VMEM((2, cols + 2 * HALO, BLOCK), BF16),
            pltpu.SemaphoreType.DMA,
            pltpu.SemaphoreType.DMA((ITERS * HALVES * 2, 16)),
            pltpu.SemaphoreType.DMA((ITERS * HALVES * 2, 16)),
            pltpu.SemaphoreType.DMA((ITERS * HALVES, 12)),
            pltpu.SemaphoreType.DMA((ITERS * HALVES, 12)),
            pltpu.SemaphoreType.DMA((2,)),
        ],
        compiler_params=pltpu.CompilerParams(
            collective_id=0, has_side_effects=True, vmem_limit_bytes=56 * 1024 * 1024
        ),
        cost_estimate=pl.CostEstimate(flops=6 * 10**9, bytes_accessed=8 * 10**6, transcendentals=0),
    )(
        arc_month,
        panels,
        observations.reshape(every, samples),
        data_weights,
        fields,
        diag_scale,
        smooth_coef,
        neighbours,
        time_coupling.reshape(1, cols),
    )


def solution(mesh):
    return jax.shard_map(
        on_device,
        mesh=mesh,
        in_specs=(
            P("month", None, "mascon"),
            P("month", None, None),
            P("month", None),
            P(),
            P("month", "mascon", None),
            P("month", "mascon"),
            P(None, "mascon"),
            P(None, "mascon"),
            P("mascon"),
        ),
        out_specs=P("month", "mascon", None),
        check_vma=False,
    )
```

```python
import functools

import jax
import jax.numpy as jnp
from jax import lax
from jax.experimental import pallas as pl
from jax.experimental.pallas import tpu as pltpu
from jax.sharding import PartitionSpec as P

MESH = pl.DeviceIdType.MESH
HALO = 64
ITERS = 2
HALVES = 2
BLOCK = 128
CHUNKS = 2
LEVELS = 32767.0
RELAX = 0.5

PEERS = (10, 6, 9, 14, 11, 5, 15, 7, 13, 2, 8, 1, 4, 3, 12)

F32, BF16, I16 = jnp.float32, jnp.bfloat16, jnp.int16


def encode(x):
    top = jnp.maximum(jnp.max(jnp.abs(x), axis=0, keepdims=True), 1e-30)
    code = jnp.round(x * (LEVELS / top)).astype(jnp.int32).astype(I16)
    return code, top * (1.0 / LEVELS)


def decode(code, scale):
    return code.astype(jnp.int32).astype(F32) * scale


def kernel(
    shape,
    arc_month,
    panels_hbm,
    obs_hbm,
    weights_hbm,
    fields_hbm,
    diag_hbm,
    coef_hbm,
    neighbours_hbm,
    coupling_hbm,
    out_hbm,
    panels,
    obs,
    weights,
    diag,
    coef,
    neighbours,
    coupling,
    result,
    turned,
    wide,
    coded,
    scales,
    states,
    every_month,
    track,
    partial,
    lane_sum,
    lane_got,
    resid,
    masked,
    grad,
    grad_code,
    grad_scale,
    grad_code_in,
    grad_scale_in,
    base,
    weight_rows,
    stencil,
    keep_rows,
    step_rows,
    time_rows,
    columns,
    split,
    load_sem,
    store_sem,
    plane_send,
    plane_recv,
    one_send,
    one_recv,
    turn_sem,
):
    cols, arcs, rows, total = shape
    blocks = cols // BLOCK
    chunk = cols // CHUNKS
    chunk_blocks = chunk // BLOCK
    every = arcs * rows
    piece = every // 16
    g, s = lax.axis_index("month"), lax.axis_index("mascon")
    core, hi = g % 2, g // 2
    z, y, x_lo = s // 8, (s // 2) % 4, s % 2
    q = z * 4 + y
    mate_month = g + 1 - 2 * core
    pair_month = (g + 2) % 4
    far_month = (mate_month + 2) % 4
    mate = (mate_month, s)
    pair = (pair_month, s)
    beside = (g, s + 1 - 2 * x_lo)
    right = (g, (s + 1) % 32)
    left = (g, (s + 31) % 32)

    def peer(d):
        return ((z + d // 4) % 4) * 4 + (y + d % 4) % 4

    def device(p):
        return (g, p * 2 + x_lo)

    across = ("pc0", "ps0", "pc1", "ps1")
    local = ("mc", "ms")
    rims = ("hl", "hr")

    barrier = pltpu.get_barrier_semaphore()

    def greet(d, carry):
        pl.semaphore_signal(barrier, inc=1, device_id=device(peer(d)), device_id_type=MESH)
        return carry

    lax.fori_loop(1, 16, greet, 0)
    for other in (mate, pair, left, right):
        pl.semaphore_signal(barrier, inc=1, device_id=other, device_id_type=MESH)

    loads = [
        pltpu.make_async_copy(
            fields_hbm.at[0, :, pl.ds(h * BLOCK, BLOCK)], wide.at[0, h, pl.ds(HALO, cols)], load_sem.at[h]
        )
        for h in range(HALVES)
    ]
    pairs = (
        (panels_hbm, panels),
        (neighbours_hbm, neighbours),
        (coef_hbm, coef),
        (diag_hbm, diag),
        (coupling_hbm, coupling),
        (weights_hbm, weights),
        (obs_hbm, obs),
    )
    loads += [pltpu.make_async_copy(src, dst, load_sem.at[HALVES + i]) for i, (src, dst) in enumerate(pairs)]
    for load in loads:
        load.start()

    names = ("pc0", "pc1", "ps0", "ps1", "fc0", "fc1", "fs0", "fs1", "gc0", "gc1", "gs0", "gs1")
    names += ("mc", "ms", "hl", "hr", "xl", "wm")
    targets = (pair, pair, pair, pair, mate, mate, mate, mate, pair, pair, pair, pair)
    targets += (mate, mate, left, right, beside, mate)

    def copy(it, h, name):
        w = wide.at[it, h]
        c = int(name[2]) if len(name) == 3 else 0
        part = pl.ds(c * chunk, chunk)
        if name[:2] == "pc":
            src = dst = coded.at[it, h, g, part]
        elif name[:2] == "ps":
            src = dst = scales.at[it, h, g, c]
        elif name[:2] == "fc":
            src = dst = coded.at[it, h, pair_month, part]
        elif name[:2] == "fs":
            src = dst = scales.at[it, h, pair_month, c]
        elif name[:2] == "gc":
            src, dst = grad_code.at[it, h, part], grad_code_in.at[it, h, part]
        elif name[:2] == "gs":
            src, dst = grad_scale.at[it, h, c], grad_scale_in.at[it, h, c]
        elif name == "mc":
            src = dst = coded.at[it, h, g]
        elif name == "ms":
            src = dst = scales.at[it, h, g]
        elif name == "hl":
            src, dst = w.at[pl.ds(HALO, HALO)], w.at[pl.ds(HALO + cols, HALO)]
        elif name == "hr":
            src, dst = w.at[pl.ds(cols, HALO)], w.at[pl.ds(0, HALO)]
        elif name == "xl":
            src, dst = lane_sum.at[it, h], lane_got.at[it, h]
        else:
            src = dst = resid.at[it, h, core]
        i = names.index(name)
        return pltpu.make_async_remote_copy(
            src_ref=src,
            dst_ref=dst,
            send_sem=one_send.at[it * HALVES + h, i],
            recv_sem=one_recv.at[it * HALVES + h, i],
            device_id=targets[i],
            device_id_type=MESH,
        )

    waited = set()

    def sent(it, h, *which):
        for name in which:
            if (it, h, name) not in waited:
                waited.add((it, h, name))
                copy(it, h, name).wait_send()

    def start(it, h, *which):
        for name in which:
            copy(it, h, name).start()

    def arrived(it, h, *which):
        for name in which:
            copy(it, h, name).wait_recv()

    def plane(it, h, phase, d, src, dst):
        return pltpu.make_async_remote_copy(
            src_ref=src,
            dst_ref=dst,
            send_sem=plane_send.at[(it * HALVES + h) * 2 + phase, d],
            recv_sem=plane_recv.at[(it * HALVES + h) * 2 + phase, d],
            device_id=device(peer(d)),
            device_id_type=MESH,
        )

    def reduce_copy(it, h, d):
        first = pl.multiple_of(peer(d) * piece, piece)
        return plane(it, h, 0, d, track.at[it, h, pl.ds(first, piece)], partial.at[it, h, d])

    def gather_copy(it, h, d):
        first = pl.multiple_of(q * piece, piece)
        own = resid.at[it, h, core, pl.ds(first, piece)]
        return plane(it, h, 1, d, own, own)

    def loop(low, high, body):
        def run(i, carry):
            body(i)
            return carry

        lax.fori_loop(low, high, run, 0)

    def over_blocks(c, body):
        loop(0, chunk_blocks, lambda b: body(b, pl.multiple_of(c * chunk + b * BLOCK, BLOCK)))

    def lane(month):
        return pl.multiple_of((((month // 2) + hi) % 2 * 2 + month % 2) * BLOCK, BLOCK)

    def encode_state(it, h, c):
        def body(b, r):
            x = wide[it, h, pl.ds(HALO + r, BLOCK), :]
            code, scale = encode(x)
            coded[it, h, g, pl.ds(r, BLOCK), :] = code
            scales[it, h, g, c, pl.ds(b, 1), :] = scale
            states[h, pl.ds(r, BLOCK), pl.ds(lane(g), BLOCK)] = x.astype(BF16)

        over_blocks(c, body)

    def unpack(it, h, month, c):
        def body(b, r):
            x = decode(coded[it, h, month, pl.ds(r, BLOCK), :], scales[it, h, month, c, pl.ds(b, 1), :])
            states[h, pl.ds(r, BLOCK), pl.ds(lane(month), BLOCK)] = x.astype(BF16)

        over_blocks(c, body)

    def predict(h, side):
        def part(i):
            r = pl.multiple_of(i * (every // 2), every // 2)
            sums = jnp.dot(
                panels[pl.ds(r, every // 2), :],
                states[h, :, pl.ds(side * 2 * BLOCK, 2 * BLOCK)],
                preferred_element_type=F32,
            )
            every_month[side * 2, pl.ds(r, every // 2), :] = sums[:, :BLOCK]
            every_month[side * 2 + 1, pl.ds(r, every // 2), :] = sums[:, BLOCK:]

        loop(0, 2, part)

    def chip_months(it, h):
        arrived(it, h, "mc", "ms")
        for c in range(CHUNKS):
            unpack(it, h, mate_month, c)
        predict(h, 0)

    def far_arrive(it, h):
        for c in range(CHUNKS):
            arrived(it, h, f"pc{c}", f"ps{c}")
            start(it, h, f"fc{c}", f"fs{c}")
            unpack(it, h, pair_month, c)

    def far_predict(it, h):
        for c in range(CHUNKS):
            arrived(it, h, f"fc{c}", f"fs{c}")
            unpack(it, h, far_month, c)
        predict(h, 1)

        def choose(a):
            month = arc_month[g * arcs + a]
            r = pl.multiple_of(a * rows, rows)
            place = (month // 2 + hi) % 2 * 2 + month % 2
            track[it, h, pl.ds(r, rows), :] = every_month[place, pl.ds(r, rows), :]

        loop(0, arcs, choose)

    def reduce_start(it, h):
        for d in PEERS:
            reduce_copy(it, h, d).start()

    def reduce_plane(it, h):
        def add(d, acc):
            reduce_copy(it, h, d).wait_recv()
            return acc + partial[it, h, d]

        own = track[it, h, pl.ds(pl.multiple_of(q * piece, piece), piece), :]
        lane_sum[it, h] = lax.fori_loop(1, 16, add, own)
        start(it, h, "xl")

    def weigh(it, h):
        own = pl.ds(pl.multiple_of(q * piece, piece), piece)
        arrived(it, h, "xl")
        full = lane_sum[it, h] + lane_got[it, h]
        seen = obs[own, pl.ds(h * BLOCK, BLOCK)].astype(F32)
        resid[it, h, core, own, :] = (weight_rows[own, :] * (full - seen)).astype(BF16)
        for d in PEERS:
            gather_copy(it, h, d).start()

    def place_resid(it, h, blk):
        def arc(a):
            month = arc_month[(hi * 2 + blk) * arcs + a]
            r = pl.multiple_of(a * rows, rows)
            w = resid[it, h, blk, pl.ds(r, rows), :].astype(F32)
            masked[blk, pl.ds(r, rows), pl.ds(0, BLOCK)] = jnp.where(month == pair_month, w, 0.0).astype(BF16)
            masked[blk, pl.ds(r, rows), pl.ds(BLOCK, BLOCK)] = jnp.where(month == g, w, 0.0).astype(BF16)

        loop(0, arcs, arc)

    def gradient_here(it, h):
        loop(1, 16, lambda d: gather_copy(it, h, d).wait_recv())
        start(it, h, "wm")
        place_resid(it, h, core)

        def part(c):
            r = pl.multiple_of(c * chunk, chunk)
            grad[h, pl.ds(r, chunk), :] = jnp.dot(
                turned[core, pl.ds(r, chunk), :], masked[core], preferred_element_type=F32
            )

        loop(0, CHUNKS, part)

    def gradient_mate(it, h):
        arrived(it, h, "wm")
        place_resid(it, h, 1 - core)
        for c in range(CHUNKS):
            part = pl.ds(c * chunk, chunk)
            grad[h, part, :] += jnp.dot(turned[1 - core, part, :], masked[1 - core], preferred_element_type=F32)

            def body(b, r):
                code, scale = encode(grad[h, pl.ds(r, BLOCK), pl.ds(0, BLOCK)])
                grad_code[it, h, pl.ds(r, BLOCK), :] = code
                grad_scale[it, h, c, pl.ds(b, 1), :] = scale

            over_blocks(c, body)
            start(it, h, f"gc{c}", f"gs{c}")

    def smooth(it, h):
        arrived(it, h, "hl", "hr")
        first = jnp.where(g == 0, 0.0, 1.0)
        last = jnp.where(g == 3, 0.0, 1.0)
        before, after = jnp.maximum(g - 1, 0), jnp.minimum(g + 1, 3)
        w = wide[it, h]
        high = w.astype(BF16)
        split[0] = high
        split[1] = (w - high.astype(F32)).astype(BF16)
        for c in range(CHUNKS):

            def body(b, r):
                high = split[0, pl.ds(r, 2 * BLOCK), :]
                window = jnp.concatenate([high, high, split[1, pl.ds(r, 2 * BLOCK), :]], axis=0)
                near = jnp.dot(stencil[c * chunk_blocks + b], window, preferred_element_type=F32)
                old = first * decode(coded[it, h, before, pl.ds(r, BLOCK), :], scales[it, h, before, c, pl.ds(b, 1), :])
                new = last * decode(coded[it, h, after, pl.ds(r, BLOCK), :], scales[it, h, after, c, pl.ds(b, 1), :])
                base[h, pl.ds(r, BLOCK), :] = (
                    wide[it, h, pl.ds(HALO + r, BLOCK), :] * keep_rows[pl.ds(r, BLOCK), :]
                    + near
                    + time_rows[pl.ds(r, BLOCK), :] * (old + new)
                )

            over_blocks(c, body)

    def store(h):
        return pltpu.make_async_copy(
            result.at[h], out_hbm.at[0, :, pl.ds(h * BLOCK, BLOCK)], store_sem.at[h]
        )

    def update(it, h):
        for c in range(CHUNKS):
            arrived(it, h, f"gc{c}", f"gs{c}")

            def body(b, r):
                theirs = decode(grad_code_in[it, h, pl.ds(r, BLOCK), :], grad_scale_in[it, h, c, pl.ds(b, 1), :])
                new = base[h, pl.ds(r, BLOCK), :] - step_rows[pl.ds(r, BLOCK), :] * (
                    grad[h, pl.ds(r, BLOCK), pl.ds(BLOCK, BLOCK)] + theirs
                )
                if it == ITERS - 1:
                    result[h, pl.ds(r, BLOCK), :] = new
                else:
                    wide[it + 1, h, pl.ds(HALO + r, BLOCK), :] = new

            over_blocks(c, body)
            if it < ITERS - 1:
                encode_state(it + 1, h, c)
                start(it + 1, h, f"pc{c}", f"ps{c}")
        if it < ITERS - 1:
            start(it + 1, h, *local, *rims)
        else:
            store(h).start()

    turn = pltpu.make_async_remote_copy(
        src_ref=turned.at[core],
        dst_ref=turned.at[core],
        send_sem=turn_sem.at[0],
        recv_sem=turn_sem.at[1],
        device_id=mate,
        device_id_type=MESH,
    )

    def prepare():
        for load in loads[HALVES:]:
            load.wait()

        def arc(a):
            r = pl.multiple_of(a * rows, rows)
            turned[core, :, pl.ds(r, rows)] = panels[pl.ds(r, rows), :].T

        loop(0, arcs, arc)
        by_row = weights[...].astype(F32).T
        for a in range(arcs):
            weight_rows[a * rows : (a + 1) * rows, :] = jnp.broadcast_to(by_row[:, a : a + 1], (rows, BLOCK))

        count = neighbours.shape[0]
        here = s * cols + lax.broadcasted_iota(jnp.int32, (count, cols), 1)
        offset = neighbours[...] - here + HALO
        offset = jnp.where(offset < 0, offset + total, offset)
        offset = jnp.where(offset >= total, offset - total, offset)
        step = RELAX / diag[...]
        near = coef[...]
        own = jnp.sum(near, axis=0, keepdims=True)
        time = coupling[...].reshape(1, cols)
        table = jnp.concatenate(
            [offset.astype(F32), near * step, step, 1.0 - step * (own + 2.0 * time), step * time, jnp.zeros_like(step)],
            axis=0,
        )
        columns[...] = table.T

        def body(b):
            r = pl.multiple_of(b * BLOCK, BLOCK)
            part = columns[pl.ds(r, BLOCK), :]
            place = (
                lax.broadcasted_iota(jnp.int32, (BLOCK, 2 * BLOCK), 1)
                - lax.broadcasted_iota(jnp.int32, (BLOCK, 2 * BLOCK), 0)
            ).astype(F32)
            band = jnp.zeros((BLOCK, 2 * BLOCK), F32)
            for n in range(count):
                band = band + jnp.where(place == part[:, n : n + 1], part[:, count + n : count + n + 1], 0.0)
            high = band.astype(BF16)
            low = (band - high.astype(F32)).astype(BF16)
            stencil[b, :, pl.ds(0, 2 * BLOCK)] = high
            stencil[b, :, pl.ds(2 * BLOCK, 2 * BLOCK)] = low
            stencil[b, :, pl.ds(4 * BLOCK, 2 * BLOCK)] = high
            for k, where in enumerate((step_rows, keep_rows, time_rows)):
                where[pl.ds(r, BLOCK), :] = jnp.broadcast_to(
                    part[:, 2 * count + k : 2 * count + k + 1], (BLOCK, BLOCK)
                )

        loop(0, blocks, body)

    def settle(it, h):
        sent(it, h, *names)
        for d in PEERS:
            reduce_copy(it, h, d).wait_send()
            gather_copy(it, h, d).wait_send()

    for h in range(HALVES):
        loads[h].wait()
        for c in range(CHUNKS):
            encode_state(0, h, c)
        if h == 0:
            pl.semaphore_wait(barrier, 19)
            start(0, 0, *across)
        start(0, h, *local)
    prepare()
    chip_months(0, 0)
    sent(0, 0, *across)
    start(0, 0, *rims)
    start(0, 1, *across, *rims)
    for it in range(ITERS):
        far_arrive(it, 0)
        far_predict(it, 0)
        reduce_start(it, 0)
        if it == 0:
            turn.start()
        else:
            settle(it - 1, 0)
        chip_months(it, 1)
        smooth(it, 0)
        far_arrive(it, 1)
        far_predict(it, 1)
        reduce_start(it, 1)
        reduce_plane(it, 0)
        smooth(it, 1)
        weigh(it, 0)
        if it == 0:
            turn.wait()
        else:
            settle(it - 1, 1)
        reduce_plane(it, 1)
        gradient_here(it, 0)
        weigh(it, 1)
        gradient_mate(it, 0)
        gradient_here(it, 1)
        gradient_mate(it, 1)
        update(it, 0)
        if it < ITERS - 1:
            chip_months(it + 1, 0)
            update(it, 1)
    settle(ITERS - 1, 0)
    update(ITERS - 1, 1)
    settle(ITERS - 1, 1)
    for h in range(HALVES):
        store(h).wait()


def on_device(panels, observations, data_weights, arc_month, fields, diag_scale, smooth_coef, neighbours, time_coupling):
    arcs, rows, cols = panels.shape
    samples = fields.shape[2]
    total = cols * lax.axis_size("mascon")
    every = arcs * rows
    piece = every // 16
    stages = (ITERS, HALVES)
    anywhere = pl.BlockSpec(memory_space=pl.ANY)
    return pl.pallas_call(
        functools.partial(kernel, (cols, arcs, rows, total)),
        out_shape=jax.ShapeDtypeStruct(fields.shape, F32),
        in_specs=[pl.BlockSpec(memory_space=pltpu.SMEM)] + [anywhere] * 8,
        out_specs=anywhere,
        scratch_shapes=[
            pltpu.VMEM((every, cols), BF16),
            pltpu.VMEM((every, samples), BF16),
            pltpu.VMEM(data_weights.shape, BF16),
            pltpu.VMEM(diag_scale.shape, F32),
            pltpu.VMEM(smooth_coef.shape, F32),
            pltpu.VMEM(neighbours.shape, jnp.int32),
            pltpu.VMEM(time_coupling.shape, F32),
            pltpu.VMEM((HALVES, cols, BLOCK), F32),
            pltpu.VMEM((2, cols, every), BF16),
            pltpu.VMEM(stages + (cols + 2 * HALO, BLOCK), F32),
            pltpu.VMEM(stages + (4, cols, BLOCK), I16),
            pltpu.VMEM(stages + (4, CHUNKS, 8, BLOCK), F32),
            pltpu.VMEM((HALVES, cols, 4 * BLOCK), BF16),
            pltpu.VMEM((4, every, BLOCK), F32),
            pltpu.VMEM(stages + (every, BLOCK), F32),
            pltpu.VMEM(stages + (16, piece, BLOCK), F32),
            pltpu.VMEM(stages + (piece, BLOCK), F32),
            pltpu.VMEM(stages + (piece, BLOCK), F32),
            pltpu.VMEM(stages + (2, every, BLOCK), BF16),
            pltpu.VMEM((2, every, 2 * BLOCK), BF16),
            pltpu.VMEM((HALVES, cols, 2 * BLOCK), F32),
            pltpu.VMEM(stages + (cols, BLOCK), I16),
            pltpu.VMEM(stages + (CHUNKS, 8, BLOCK), F32),
            pltpu.VMEM(stages + (cols, BLOCK), I16),
            pltpu.VMEM(stages + (CHUNKS, 8, BLOCK), F32),
            pltpu.VMEM((HALVES, cols, BLOCK), F32),
            pltpu.VMEM((every, BLOCK), F32),
            pltpu.VMEM((cols // BLOCK, BLOCK, 6 * BLOCK), BF16),
            pltpu.VMEM((cols, BLOCK), F32),
            pltpu.VMEM((cols, BLOCK), F32),
            pltpu.VMEM((cols, BLOCK), F32),
            pltpu.VMEM((cols, 16), F32),
            pltpu.VMEM((2, cols + 2 * HALO, BLOCK), BF16),
            pltpu.SemaphoreType.DMA((HALVES + 7,)),
            pltpu.SemaphoreType.DMA((HALVES,)),
            pltpu.SemaphoreType.DMA((ITERS * HALVES * 2, 16)),
            pltpu.SemaphoreType.DMA((ITERS * HALVES * 2, 16)),
            pltpu.SemaphoreType.DMA((ITERS * HALVES, 18)),
            pltpu.SemaphoreType.DMA((ITERS * HALVES, 18)),
            pltpu.SemaphoreType.DMA((2,)),
        ],
        compiler_params=pltpu.CompilerParams(
            collective_id=0, has_side_effects=True, vmem_limit_bytes=56 * 1024 * 1024
        ),
        cost_estimate=pl.CostEstimate(flops=6 * 10**9, bytes_accessed=8 * 10**6, transcendentals=0),
    )(
        arc_month,
        panels.reshape(every, cols),
        observations.reshape(every, samples),
        data_weights,
        fields,
        diag_scale,
        smooth_coef,
        neighbours,
        time_coupling,
    )


def solution(mesh):
    return jax.shard_map(
        on_device,
        mesh=mesh,
        in_specs=(
            P("month", None, "mascon"),
            P("month", None, None),
            P("month", None),
            P(),
            P("month", "mascon", None),
            P("month", "mascon"),
            P(None, "mascon"),
            P(None, "mascon"),
            P("mascon"),
        ),
        out_specs=P("month", "mascon", None),
        check_vma=False,
    )
```

```python
import functools

import jax
import jax.numpy as jnp
from jax import lax
from jax.experimental import pallas as pl
from jax.experimental.pallas import tpu as pltpu
from jax.sharding import PartitionSpec as P

MESH = pl.DeviceIdType.MESH
HALO = 64
ITERS = 2
HALVES = 2
BLOCK = 128
CHUNKS = 2
LEVELS = 32767.0
RELAX = 0.5

PEERS = (10, 6, 9, 14, 11, 5, 15, 7, 13, 2, 8, 1, 4, 3, 12)

F32, BF16, I16 = jnp.float32, jnp.bfloat16, jnp.int16


FINE = 256.0
MARK = 16


def level_code(top):
    return jnp.ceil(jnp.log2(jnp.maximum(top, 1e-30)) * FINE) + 1.0


def level(code):
    return jnp.exp2(code * (1.0 / FINE))


def to_code(x):
    return x.astype(jnp.int32).astype(I16)


def to_float(code):
    return code.astype(jnp.int32).astype(F32)


def kernel(
    shape,
    arc_hbm,
    panels_hbm,
    obs_hbm,
    weights_hbm,
    fields_hbm,
    diag_hbm,
    coef_hbm,
    neighbours_hbm,
    coupling_hbm,
    out_hbm,
    arc_month,
    panels,
    obs,
    weights,
    diag,
    coef,
    neighbours,
    coupling,
    result,
    turned,
    wide,
    coded,
    rim,
    tops,
    gains,
    units,
    states,
    every_month,
    track,
    partial,
    lane_sum,
    lane_got,
    resid,
    masked,
    grad,
    grad_code,
    grad_code_in,
    base,
    weight_rows,
    stencil,
    keep_rows,
    step_rows,
    time_rows,
    columns,
    split,
    load_sem,
    store_sem,
    plane_send,
    plane_recv,
    one_send,
    one_recv,
    turn_sem,
):
    cols, arcs, rows, total = shape
    blocks = cols // BLOCK
    chunk = cols // CHUNKS
    chunk_blocks = chunk // BLOCK
    every = arcs * rows
    piece = every // 16
    g, s = lax.axis_index("month"), lax.axis_index("mascon")
    core, hi = g % 2, g // 2
    z, y, x_lo = s // 8, (s // 2) % 4, s % 2
    q = z * 4 + y
    mate_month = g + 1 - 2 * core
    pair_month = (g + 2) % 4
    far_month = (mate_month + 2) % 4
    mate = (mate_month, s)
    pair = (pair_month, s)
    beside = (g, s + 1 - 2 * x_lo)
    right = (g, (s + 1) % 32)
    left = (g, (s + 31) % 32)

    def peer(d):
        return ((z + d // 4) % 4) * 4 + (y + d % 4) % 4

    def device(p):
        return (g, p * 2 + x_lo)

    across = ("pc0", "pc1")
    local = ("mc",)
    rims = ("hl", "hr")

    tops[...] = jnp.ones_like(tops)

    barrier = pltpu.get_barrier_semaphore()

    def greet(d, carry):
        pl.semaphore_signal(barrier, inc=1, device_id=device(peer(d)), device_id_type=MESH)
        return carry

    lax.fori_loop(1, 16, greet, 0)
    for other in (mate, pair, left, right):
        pl.semaphore_signal(barrier, inc=1, device_id=other, device_id_type=MESH)

    loads = [
        pltpu.make_async_copy(
            fields_hbm.at[0, :, pl.ds(h * BLOCK, BLOCK)], wide.at[0, h, pl.ds(HALO, cols)], load_sem.at[h]
        )
        for h in range(HALVES)
    ]
    pairs = (
        (arc_hbm, arc_month),
        (panels_hbm, panels),
        (neighbours_hbm, neighbours),
        (coef_hbm, coef),
        (diag_hbm, diag),
        (coupling_hbm, coupling),
        (weights_hbm, weights),
        (obs_hbm, obs),
    )
    loads += [pltpu.make_async_copy(src, dst, load_sem.at[HALVES + i]) for i, (src, dst) in enumerate(pairs)]
    for load in loads:
        load.start()

    names = ("pc0", "pc1", "fc0", "fc1", "gc0", "gc1", "mc", "hl", "hr", "xl", "wm")
    targets = (pair, pair, mate, mate, pair, pair, mate, left, right, beside, mate)
    coded_chunk = chunk + MARK
    marks = (pl.ds(0, MARK), pl.ds(MARK + cols, MARK))

    def copy(it, h, name):
        c = int(name[2]) if len(name) == 3 else 0
        part = pl.ds(c * coded_chunk, coded_chunk)
        if name[:2] == "pc":
            src = dst = coded.at[it, h, g, part]
        elif name[:2] == "fc":
            src = dst = coded.at[it, h, pair_month, part]
        elif name[:2] == "gc":
            src, dst = grad_code.at[it, h, part], grad_code_in.at[it, h, part]
        elif name == "mc":
            src = dst = coded.at[it, h, g]
        elif name == "hl":
            src, dst = coded.at[it, h, g, pl.ds(0, HALO + MARK)], rim.at[it, h, 1]
        elif name == "hr":
            src, dst = coded.at[it, h, g, pl.ds(MARK + cols - HALO, HALO + MARK)], rim.at[it, h, 0]
        elif name == "xl":
            src, dst = lane_sum.at[it, h], lane_got.at[it, h]
        else:
            src = dst = resid.at[it, h, core]
        i = names.index(name)
        return pltpu.make_async_remote_copy(
            src_ref=src,
            dst_ref=dst,
            send_sem=one_send.at[it * HALVES + h, i],
            recv_sem=one_recv.at[it * HALVES + h, i],
            device_id=targets[i],
            device_id_type=MESH,
        )

    waited = set()

    def sent(it, h, *which):
        for name in which:
            if (it, h, name) not in waited:
                waited.add((it, h, name))
                copy(it, h, name).wait_send()

    def start(it, h, *which):
        for name in which:
            copy(it, h, name).start()

    def arrived(it, h, *which):
        for name in which:
            copy(it, h, name).wait_recv()

    def plane(it, h, phase, d, src, dst):
        return pltpu.make_async_remote_copy(
            src_ref=src,
            dst_ref=dst,
            send_sem=plane_send.at[(it * HALVES + h) * 2 + phase, d],
            recv_sem=plane_recv.at[(it * HALVES + h) * 2 + phase, d],
            device_id=device(peer(d)),
            device_id_type=MESH,
        )

    def reduce_copy(it, h, d):
        return plane(it, h, 0, d, track.at[it, h, peer(d)], partial.at[it, h, d])

    def gather_copy(it, h, d):
        first = pl.multiple_of(q * piece, piece)
        own = resid.at[it, h, core, pl.ds(first, piece)]
        return plane(it, h, 1, d, own, own)

    def loop(low, high, body):
        def run(i, carry):
            body(i)
            return carry

        lax.fori_loop(low, high, run, 0)

    def over_blocks(c, body):
        loop(0, chunk_blocks, lambda b: body(b, pl.multiple_of(c * chunk + b * BLOCK, BLOCK)))

    def lane(month):
        return pl.multiple_of((((month // 2) + hi) % 2 * 2 + month % 2) * BLOCK, BLOCK)

    def data(r, size=BLOCK):
        return pl.ds(pl.multiple_of(MARK + r, MARK), size)

    def encode(c, read, ref):
        def peak(b, r):
            tops[pl.ds(b, 1), :] = jnp.max(jnp.abs(read(r)), axis=0, keepdims=True)

        def put(b, r):
            ref[data(r), :] = to_code(jnp.round(read(r) * gains[pl.ds(b, 1), :]))

        over_blocks(c, peak)
        code = level_code(tops[...])
        ref[marks[c], :] = to_code(code)
        gains[...] = LEVELS / level(code)
        over_blocks(c, put)

    def set_units(i, c, ref):
        units[i] = level(to_float(ref[marks[c], :])) * (1.0 / LEVELS)

    def decode(i, ref, b, r):
        return to_float(ref[data(r), :]) * units[i, pl.ds(b, 1), :]

    def encode_state(it, h, c):
        encode(c, lambda r: wide[it, h, pl.ds(HALO + r, BLOCK), :], coded.at[it, h, g])

        def body(b, r):
            states[h, pl.ds(r, BLOCK), pl.ds(lane(g), BLOCK)] = wide[it, h, pl.ds(HALO + r, BLOCK), :].astype(BF16)

        over_blocks(c, body)

    def unpack(it, h, month, c):
        ref = coded.at[it, h, month]
        set_units(0, c, ref)

        def body(b, r):
            states[h, pl.ds(r, BLOCK), pl.ds(lane(month), BLOCK)] = decode(0, ref, b, r).astype(BF16)

        over_blocks(c, body)

    def predict(h, side):
        def part(i):
            r = pl.multiple_of(i * (every // 2), every // 2)
            sums = jnp.dot(
                panels[pl.ds(r, every // 2), :],
                states[h, :, pl.ds(side * 2 * BLOCK, 2 * BLOCK)],
                preferred_element_type=F32,
            )
            every_month[side * 2, pl.ds(r, every // 2), :] = sums[:, :BLOCK]
            every_month[side * 2 + 1, pl.ds(r, every // 2), :] = sums[:, BLOCK:]

        loop(0, 2, part)

    def chip_months(it, h):
        arrived(it, h, "mc")
        for c in range(CHUNKS):
            unpack(it, h, mate_month, c)
        predict(h, 0)

    def far_arrive(it, h):
        for c in range(CHUNKS):
            arrived(it, h, f"pc{c}")
            start(it, h, f"fc{c}")
            unpack(it, h, pair_month, c)

    def far_predict(it, h):
        for c in range(CHUNKS):
            arrived(it, h, f"fc{c}")
            unpack(it, h, far_month, c)
        predict(h, 1)

        def choose(a):
            month = arc_month[g * arcs + a]
            r = pl.multiple_of(a * rows, rows)
            place = (month // 2 + hi) % 2 * 2 + month % 2
            for u in range(rows // piece):
                sums = every_month[place, pl.ds(r + u * piece, piece), :]
                code = level_code(jnp.max(jnp.abs(sums), axis=0, keepdims=True))
                p = a * (rows // piece) + u
                track[it, h, p, pl.ds(0, piece), :] = to_code(jnp.round(sums * (LEVELS / level(code))))
                track[it, h, p, pl.ds(piece, MARK), :] = to_code(jnp.broadcast_to(code, (MARK, BLOCK)))

        loop(0, arcs, choose)

    def reduce_start(it, h):
        for d in PEERS:
            reduce_copy(it, h, d).start()

    def reduce_plane(it, h):
        def value(code):
            both = to_float(code)
            return both[:piece] * (level(both[piece : piece + 1]) * (1.0 / LEVELS))

        def add(d, acc):
            reduce_copy(it, h, d).wait_recv()
            return acc + value(partial[it, h, d])

        lane_sum[it, h] = lax.fori_loop(1, 16, add, value(track[it, h, q]))
        start(it, h, "xl")

    def weigh(it, h):
        own = pl.ds(pl.multiple_of(q * piece, piece), piece)
        arrived(it, h, "xl")
        full = lane_sum[it, h] + lane_got[it, h]
        seen = obs[own, pl.ds(h * BLOCK, BLOCK)].astype(F32)
        resid[it, h, core, own, :] = (weight_rows[own, :] * (full - seen)).astype(BF16)
        for d in PEERS:
            gather_copy(it, h, d).start()

    def place_resid(it, h, blk):
        def arc(a):
            month = arc_month[(hi * 2 + blk) * arcs + a]
            r = pl.multiple_of(a * rows, rows)
            w = resid[it, h, blk, pl.ds(r, rows), :].astype(F32)
            masked[blk, pl.ds(r, rows), pl.ds(0, BLOCK)] = jnp.where(month == pair_month, w, 0.0).astype(BF16)
            masked[blk, pl.ds(r, rows), pl.ds(BLOCK, BLOCK)] = jnp.where(month == g, w, 0.0).astype(BF16)

        loop(0, arcs, arc)

    def gradient_here(it, h):
        loop(1, 16, lambda d: gather_copy(it, h, d).wait_recv())
        start(it, h, "wm")
        place_resid(it, h, core)

        def part(c):
            r = pl.multiple_of(c * chunk, chunk)
            grad[h, pl.ds(r, chunk), :] = jnp.dot(
                turned[core, pl.ds(r, chunk), :], masked[core], preferred_element_type=F32
            )

        loop(0, CHUNKS, part)

    def gradient_mate(it, h):
        arrived(it, h, "wm")
        place_resid(it, h, 1 - core)
        for c in range(CHUNKS):
            part = pl.ds(c * chunk, chunk)
            grad[h, part, :] += jnp.dot(turned[1 - core, part, :], masked[1 - core], preferred_element_type=F32)

            encode(c, lambda r: grad[h, pl.ds(r, BLOCK), pl.ds(0, BLOCK)], grad_code.at[it, h])
            start(it, h, f"gc{c}")

    def smooth(it, h):
        arrived(it, h, "hl", "hr")
        first = jnp.where(g == 0, 0.0, 1.0)
        last = jnp.where(g == 3, 0.0, 1.0)
        before, after = jnp.maximum(g - 1, 0), jnp.minimum(g + 1, 3)
        rims_in = to_float(rim[it, h, 0]), to_float(rim[it, h, 1])
        unit = level(rims_in[0][HALO + chunk_blocks - 1 : HALO + chunk_blocks]) * (1.0 / LEVELS)
        wide[it, h, pl.ds(0, HALO), :] = rims_in[0][:HALO] * unit
        unit = level(rims_in[1][:1]) * (1.0 / LEVELS)
        wide[it, h, pl.ds(HALO + cols, HALO), :] = rims_in[1][MARK:] * unit
        w = wide[it, h]
        high = w.astype(BF16)
        split[0] = high
        split[1] = (w - high.astype(F32)).astype(BF16)
        for c in range(CHUNKS):
            set_units(0, c, coded.at[it, h, before])
            set_units(1, c, coded.at[it, h, after])

            def body(b, r):
                high = split[0, pl.ds(r, 2 * BLOCK), :]
                window = jnp.concatenate([high, high, split[1, pl.ds(r, 2 * BLOCK), :]], axis=0)
                near = jnp.dot(stencil[c * chunk_blocks + b], window, preferred_element_type=F32)
                old = first * decode(0, coded.at[it, h, before], b, r)
                new = last * decode(1, coded.at[it, h, after], b, r)
                base[h, pl.ds(r, BLOCK), :] = (
                    wide[it, h, pl.ds(HALO + r, BLOCK), :] * keep_rows[pl.ds(r, BLOCK), :]
                    + near
                    + time_rows[pl.ds(r, BLOCK), :] * (old + new)
                )

            over_blocks(c, body)

    def store(h, c):
        part = pl.ds(c * chunk, chunk)
        return pltpu.make_async_copy(
            result.at[h, part], out_hbm.at[0, part, pl.ds(h * BLOCK, BLOCK)], store_sem.at[h, c]
        )

    def update(it, h):
        for c in range(CHUNKS):
            arrived(it, h, f"gc{c}")
            set_units(0, c, grad_code_in.at[it, h])

            def body(b, r):
                theirs = decode(0, grad_code_in.at[it, h], b, r)
                new = base[h, pl.ds(r, BLOCK), :] - step_rows[pl.ds(r, BLOCK), :] * (
                    grad[h, pl.ds(r, BLOCK), pl.ds(BLOCK, BLOCK)] + theirs
                )
                if it == ITERS - 1:
                    result[h, pl.ds(r, BLOCK), :] = new
                else:
                    wide[it + 1, h, pl.ds(HALO + r, BLOCK), :] = new

            over_blocks(c, body)
            if it < ITERS - 1:
                encode_state(it + 1, h, c)
                start(it + 1, h, f"pc{c}")
            else:
                store(h, c).start()
        if it < ITERS - 1:
            start(it + 1, h, *local, *rims)

    turn = pltpu.make_async_remote_copy(
        src_ref=turned.at[core],
        dst_ref=turned.at[core],
        send_sem=turn_sem.at[0],
        recv_sem=turn_sem.at[1],
        device_id=mate,
        device_id_type=MESH,
    )

    def prepare():
        for load in loads[HALVES:]:
            load.wait()

        def arc(a):
            r = pl.multiple_of(a * rows, rows)
            turned[core, :, pl.ds(r, rows)] = panels[pl.ds(r, rows), :].T

        loop(0, arcs, arc)
        by_row = weights[...].astype(F32).T
        for a in range(arcs):
            weight_rows[a * rows : (a + 1) * rows, :] = jnp.broadcast_to(by_row[:, a : a + 1], (rows, BLOCK))

        count = neighbours.shape[0]
        here = s * cols + lax.broadcasted_iota(jnp.int32, (count, cols), 1)
        offset = neighbours[...] - here + HALO
        offset = jnp.where(offset < 0, offset + total, offset)
        offset = jnp.where(offset >= total, offset - total, offset)
        step = RELAX / diag[...]
        near = coef[...]
        own = jnp.sum(near, axis=0, keepdims=True)
        time = coupling[...].reshape(1, cols)
        table = jnp.concatenate(
            [offset.astype(F32), near * step, step, 1.0 - step * (own + 2.0 * time), step * time, jnp.zeros_like(step)],
            axis=0,
        )
        columns[...] = table.T

        def body(b):
            r = pl.multiple_of(b * BLOCK, BLOCK)
            part = columns[pl.ds(r, BLOCK), :]
            place = (
                lax.broadcasted_iota(jnp.int32, (BLOCK, 2 * BLOCK), 1)
                - lax.broadcasted_iota(jnp.int32, (BLOCK, 2 * BLOCK), 0)
            ).astype(F32)
            band = jnp.zeros((BLOCK, 2 * BLOCK), F32)
            for n in range(count):
                band = band + jnp.where(place == part[:, n : n + 1], part[:, count + n : count + n + 1], 0.0)
            high = band.astype(BF16)
            low = (band - high.astype(F32)).astype(BF16)
            stencil[b, :, pl.ds(0, 2 * BLOCK)] = high
            stencil[b, :, pl.ds(2 * BLOCK, 2 * BLOCK)] = low
            stencil[b, :, pl.ds(4 * BLOCK, 2 * BLOCK)] = high
            for k, where in enumerate((step_rows, keep_rows, time_rows)):
                where[pl.ds(r, BLOCK), :] = jnp.broadcast_to(
                    part[:, 2 * count + k : 2 * count + k + 1], (BLOCK, BLOCK)
                )

        loop(0, blocks, body)

    def settle(it, h):
        sent(it, h, *names)
        for d in PEERS:
            reduce_copy(it, h, d).wait_send()
            gather_copy(it, h, d).wait_send()

    for h in range(HALVES):
        loads[h].wait()
        for c in range(CHUNKS):
            encode_state(0, h, c)
        if h == 0:
            pl.semaphore_wait(barrier, 19)
            start(0, 0, *across)
        start(0, h, *local)
    prepare()
    chip_months(0, 0)
    sent(0, 0, *across)
    start(0, 0, *rims)
    start(0, 1, *across, *rims)
    for it in range(ITERS):
        far_arrive(it, 0)
        far_predict(it, 0)
        reduce_start(it, 0)
        if it == 0:
            turn.start()
        else:
            settle(it - 1, 0)
        chip_months(it, 1)
        smooth(it, 0)
        far_arrive(it, 1)
        far_predict(it, 1)
        reduce_start(it, 1)
        reduce_plane(it, 0)
        weigh(it, 0)
        smooth(it, 1)
        if it == 0:
            turn.wait()
        else:
            settle(it - 1, 1)
        reduce_plane(it, 1)
        gradient_here(it, 0)
        weigh(it, 1)
        gradient_mate(it, 0)
        gradient_here(it, 1)
        gradient_mate(it, 1)
        update(it, 0)
        if it < ITERS - 1:
            chip_months(it + 1, 0)
            update(it, 1)
    settle(ITERS - 1, 0)
    update(ITERS - 1, 1)
    settle(ITERS - 1, 1)
    for h in range(HALVES):
        for c in range(CHUNKS):
            store(h, c).wait()


def on_device(panels, observations, data_weights, arc_month, fields, diag_scale, smooth_coef, neighbours, time_coupling):
    arcs, rows, cols = panels.shape
    samples = fields.shape[2]
    total = cols * lax.axis_size("mascon")
    every = arcs * rows
    piece = every // 16
    stages = (ITERS, HALVES)
    anywhere = pl.BlockSpec(memory_space=pl.ANY)
    return pl.pallas_call(
        functools.partial(kernel, (cols, arcs, rows, total)),
        out_shape=jax.ShapeDtypeStruct(fields.shape, F32),
        in_specs=[anywhere] * 9,
        out_specs=anywhere,
        scratch_shapes=[
            pltpu.SMEM(arc_month.shape, jnp.int32),
            pltpu.VMEM((every, cols), BF16),
            pltpu.VMEM((every, samples), BF16),
            pltpu.VMEM(data_weights.shape, BF16),
            pltpu.VMEM(diag_scale.shape, F32),
            pltpu.VMEM(smooth_coef.shape, F32),
            pltpu.VMEM(neighbours.shape, jnp.int32),
            pltpu.VMEM(time_coupling.shape, F32),
            pltpu.VMEM((HALVES, cols, BLOCK), F32),
            pltpu.VMEM((2, cols, every), BF16),
            pltpu.VMEM(stages + (cols + 2 * HALO, BLOCK), F32),
            pltpu.VMEM(stages + (4, cols + CHUNKS * MARK, BLOCK), I16),
            pltpu.VMEM(stages + (2, HALO + MARK, BLOCK), I16),
            pltpu.VMEM((MARK, BLOCK), F32),
            pltpu.VMEM((MARK, BLOCK), F32),
            pltpu.VMEM((2, MARK, BLOCK), F32),
            pltpu.VMEM((HALVES, cols, 4 * BLOCK), BF16),
            pltpu.VMEM((4, every, BLOCK), F32),
            pltpu.VMEM(stages + (16, piece + MARK, BLOCK), I16),
            pltpu.VMEM(stages + (16, piece + MARK, BLOCK), I16),
            pltpu.VMEM(stages + (piece, BLOCK), F32),
            pltpu.VMEM(stages + (piece, BLOCK), F32),
            pltpu.VMEM(stages + (2, every, BLOCK), BF16),
            pltpu.VMEM((2, every, 2 * BLOCK), BF16),
            pltpu.VMEM((HALVES, cols, 2 * BLOCK), F32),
            pltpu.VMEM(stages + (cols + CHUNKS * MARK, BLOCK), I16),
            pltpu.VMEM(stages + (cols + CHUNKS * MARK, BLOCK), I16),
            pltpu.VMEM((HALVES, cols, BLOCK), F32),
            pltpu.VMEM((every, BLOCK), F32),
            pltpu.VMEM((cols // BLOCK, BLOCK, 6 * BLOCK), BF16),
            pltpu.VMEM((cols, BLOCK), F32),
            pltpu.VMEM((cols, BLOCK), F32),
            pltpu.VMEM((cols, BLOCK), F32),
            pltpu.VMEM((cols, 16), F32),
            pltpu.VMEM((2, cols + 2 * HALO, BLOCK), BF16),
            pltpu.SemaphoreType.DMA((HALVES + 8,)),
            pltpu.SemaphoreType.DMA((HALVES, CHUNKS)),
            pltpu.SemaphoreType.DMA((ITERS * HALVES * 2, 16)),
            pltpu.SemaphoreType.DMA((ITERS * HALVES * 2, 16)),
            pltpu.SemaphoreType.DMA((ITERS * HALVES, 11)),
            pltpu.SemaphoreType.DMA((ITERS * HALVES, 11)),
            pltpu.SemaphoreType.DMA((2,)),
        ],
        compiler_params=pltpu.CompilerParams(
            collective_id=0, has_side_effects=True, vmem_limit_bytes=56 * 1024 * 1024
        ),
        cost_estimate=pl.CostEstimate(flops=6 * 10**9, bytes_accessed=8 * 10**6, transcendentals=0),
    )(
        arc_month,
        panels.reshape(every, cols),
        observations.reshape(every, samples),
        data_weights,
        fields,
        diag_scale,
        smooth_coef,
        neighbours,
        time_coupling,
    )


def solution(mesh):
    return jax.shard_map(
        on_device,
        mesh=mesh,
        in_specs=(
            P("month", None, "mascon"),
            P("month", None, None),
            P("month", None),
            P(),
            P("month", "mascon", None),
            P("month", "mascon"),
            P(None, "mascon"),
            P(None, "mascon"),
            P("mascon"),
        ),
        out_specs=P("month", "mascon", None),
        check_vma=False,
    )
```

```python
import functools

import jax
import jax.numpy as jnp
from jax import lax
from jax.experimental import pallas as pl
from jax.experimental.pallas import tpu as pltpu
from jax.sharding import PartitionSpec as P

MESH = pl.DeviceIdType.MESH
HALO = 64
ITERS = 2
HALVES = 2
BLOCK = 128
CHUNKS = 2
LEVELS = 32767.0
RELAX = 0.5

PEERS = (10, 6, 9, 14, 11, 5, 15, 7, 13, 2, 8, 1, 4, 3, 12)

F32, BF16, I16 = jnp.float32, jnp.bfloat16, jnp.int16


FINE = 256.0
MARK = 16


def level_code(top):
    return jnp.ceil(jnp.log2(jnp.maximum(top, 1e-30)) * FINE) + 1.0


def level(code):
    return jnp.exp2(code * (1.0 / FINE))


def to_code(x):
    return x.astype(jnp.int32).astype(I16)


def to_float(code):
    return code.astype(jnp.int32).astype(F32)


def kernel(
    shape,
    arc_hbm,
    panels_hbm,
    obs_hbm,
    weights_hbm,
    fields_hbm,
    diag_hbm,
    coef_hbm,
    neighbours_hbm,
    coupling_hbm,
    out_hbm,
    arc_month,
    panels,
    obs,
    weights,
    diag,
    coef,
    neighbours,
    coupling,
    result,
    turned,
    wide,
    coded,
    rim,
    tops,
    gains,
    units,
    states,
    every_month,
    track,
    partial,
    lane_sum,
    lane_got,
    resid,
    masked,
    grad,
    grad_code,
    grad_code_in,
    base,
    weight_rows,
    stencil,
    keep_rows,
    step_rows,
    time_rows,
    columns,
    split,
    load_sem,
    store_sem,
    plane_send,
    plane_recv,
    one_send,
    one_recv,
    turn_sem,
):
    cols, arcs, rows, total = shape
    blocks = cols // BLOCK
    chunk = cols // CHUNKS
    chunk_blocks = chunk // BLOCK
    every = arcs * rows
    piece = every // 16
    g, s = lax.axis_index("month"), lax.axis_index("mascon")
    core, hi = g % 2, g // 2
    z, y, x_lo = s // 8, (s // 2) % 4, s % 2
    q = z * 4 + y
    mate_month = g + 1 - 2 * core
    pair_month = (g + 2) % 4
    far_month = (mate_month + 2) % 4
    mate = (mate_month, s)
    pair = (pair_month, s)
    beside = (g, s + 1 - 2 * x_lo)
    right = (g, (s + 1) % 32)
    left = (g, (s + 31) % 32)

    def peer(d):
        return ((z + d // 4) % 4) * 4 + (y + d % 4) % 4

    def device(p):
        return (g, p * 2 + x_lo)

    across = ("pc0", "pc1")
    local = ("mc",)
    rims = ("hl", "hr")

    tops[...] = jnp.ones_like(tops)

    barrier = pltpu.get_barrier_semaphore()

    def greet(d, carry):
        pl.semaphore_signal(barrier, inc=1, device_id=device(peer(d)), device_id_type=MESH)
        return carry

    lax.fori_loop(1, 16, greet, 0)
    for other in (mate, pair, left, right):
        pl.semaphore_signal(barrier, inc=1, device_id=other, device_id_type=MESH)

    loads = [
        pltpu.make_async_copy(
            fields_hbm.at[0, :, pl.ds(h * BLOCK, BLOCK)], wide.at[0, h, pl.ds(HALO, cols)], load_sem.at[h]
        )
        for h in range(HALVES)
    ]
    pairs = (
        (arc_hbm, arc_month),
        (panels_hbm, panels),
        (neighbours_hbm, neighbours),
        (coef_hbm, coef),
        (diag_hbm, diag),
        (coupling_hbm, coupling),
        (weights_hbm, weights),
        (obs_hbm, obs),
    )
    loads += [pltpu.make_async_copy(src, dst, load_sem.at[HALVES + i]) for i, (src, dst) in enumerate(pairs)]
    for load in loads:
        load.start()

    names = ("pc0", "pc1", "fc0", "fc1", "gc0", "gc1", "mc", "hl", "hr", "xl", "wm")
    targets = (pair, pair, mate, mate, pair, pair, mate, left, right, beside, mate)
    coded_chunk = chunk + MARK
    marks = (pl.ds(0, MARK), pl.ds(MARK + cols, MARK))

    def copy(it, h, name):
        c = int(name[2]) if len(name) == 3 else 0
        part = pl.ds(c * coded_chunk, coded_chunk)
        if name[:2] == "pc":
            src = dst = coded.at[it, h, g, part]
        elif name[:2] == "fc":
            src = dst = coded.at[it, h, pair_month, part]
        elif name[:2] == "gc":
            src, dst = grad_code.at[it, h, part], grad_code_in.at[it, h, part]
        elif name == "mc":
            src = dst = coded.at[it, h, g]
        elif name == "hl":
            src, dst = coded.at[it, h, g, pl.ds(0, HALO + MARK)], rim.at[it, h, 1]
        elif name == "hr":
            src, dst = coded.at[it, h, g, pl.ds(MARK + cols - HALO, HALO + MARK)], rim.at[it, h, 0]
        elif name == "xl":
            src, dst = lane_sum.at[it, h], lane_got.at[it, h]
        else:
            src = dst = resid.at[it, h, core]
        i = names.index(name)
        return pltpu.make_async_remote_copy(
            src_ref=src,
            dst_ref=dst,
            send_sem=one_send.at[it * HALVES + h, i],
            recv_sem=one_recv.at[it * HALVES + h, i],
            device_id=targets[i],
            device_id_type=MESH,
        )

    waited = set()

    def sent(it, h, *which):
        for name in which:
            if (it, h, name) not in waited:
                waited.add((it, h, name))
                copy(it, h, name).wait_send()

    def start(it, h, *which):
        for name in which:
            copy(it, h, name).start()

    def arrived(it, h, *which):
        for name in which:
            copy(it, h, name).wait_recv()

    def plane(it, h, phase, d, src, dst):
        return pltpu.make_async_remote_copy(
            src_ref=src,
            dst_ref=dst,
            send_sem=plane_send.at[(it * HALVES + h) * 2 + phase, d],
            recv_sem=plane_recv.at[(it * HALVES + h) * 2 + phase, d],
            device_id=device(peer(d)),
            device_id_type=MESH,
        )

    def reduce_copy(it, h, d):
        return plane(it, h, 0, d, track.at[it, h, peer(d)], partial.at[it, h, d])

    def gather_copy(it, h, d):
        first = pl.multiple_of(q * piece, piece)
        own = resid.at[it, h, core, pl.ds(first, piece)]
        return plane(it, h, 1, d, own, own)

    def loop(low, high, body):
        def run(i, carry):
            body(i)
            return carry

        lax.fori_loop(low, high, run, 0)

    def over_blocks(c, body):
        loop(0, chunk_blocks, lambda b: body(b, pl.multiple_of(c * chunk + b * BLOCK, BLOCK)))

    def lane(month):
        return pl.multiple_of((((month // 2) + hi) % 2 * 2 + month % 2) * BLOCK, BLOCK)

    def data(r, size=BLOCK):
        return pl.ds(pl.multiple_of(MARK + r, MARK), size)

    def encode(c, read, ref):
        def peak(b, r):
            tops[pl.ds(b, 1), :] = jnp.max(jnp.abs(read(r)), axis=0, keepdims=True)

        def put(b, r):
            ref[data(r), :] = to_code(jnp.round(read(r) * gains[pl.ds(b, 1), :]))

        over_blocks(c, peak)
        code = level_code(tops[...])
        ref[marks[c], :] = to_code(code)
        gains[...] = LEVELS / level(code)
        over_blocks(c, put)

    def set_units(i, c, ref):
        units[i] = level(to_float(ref[marks[c], :])) * (1.0 / LEVELS)

    def decode(i, ref, b, r):
        return to_float(ref[data(r), :]) * units[i, pl.ds(b, 1), :]

    def encode_state(it, h, c):
        encode(c, lambda r: wide[it, h, pl.ds(HALO + r, BLOCK), :], coded.at[it, h, g])

        def body(b, r):
            states[h, pl.ds(r, BLOCK), pl.ds(lane(g), BLOCK)] = wide[it, h, pl.ds(HALO + r, BLOCK), :].astype(BF16)

        over_blocks(c, body)

    def unpack(it, h, month, c):
        ref = coded.at[it, h, month]
        set_units(0, c, ref)

        def body(b, r):
            states[h, pl.ds(r, BLOCK), pl.ds(lane(month), BLOCK)] = decode(0, ref, b, r).astype(BF16)

        over_blocks(c, body)

    def predict(h, side):
        def part(i):
            r = pl.multiple_of(i * (every // 2), every // 2)
            sums = jnp.dot(
                panels[pl.ds(r, every // 2), :],
                states[h, :, pl.ds(side * 2 * BLOCK, 2 * BLOCK)],
                preferred_element_type=F32,
            )
            every_month[side * 2, pl.ds(r, every // 2), :] = sums[:, :BLOCK]
            every_month[side * 2 + 1, pl.ds(r, every // 2), :] = sums[:, BLOCK:]

        loop(0, 2, part)

    def chip_months(it, h):
        arrived(it, h, "mc")
        for c in range(CHUNKS):
            unpack(it, h, mate_month, c)
        predict(h, 0)

    def far_arrive(it, h):
        for c in range(CHUNKS):
            arrived(it, h, f"pc{c}")
            start(it, h, f"fc{c}")
            unpack(it, h, pair_month, c)

    def far_predict(it, h):
        for c in range(CHUNKS):
            arrived(it, h, f"fc{c}")
            unpack(it, h, far_month, c)
        predict(h, 1)

        def choose(a):
            month = arc_month[g * arcs + a]
            r = pl.multiple_of(a * rows, rows)
            place = (month // 2 + hi) % 2 * 2 + month % 2
            for u in range(rows // piece):
                sums = every_month[place, pl.ds(r + u * piece, piece), :]
                code = level_code(jnp.max(jnp.abs(sums), axis=0, keepdims=True))
                p = a * (rows // piece) + u
                track[it, h, p, pl.ds(0, piece), :] = to_code(jnp.round(sums * (LEVELS / level(code))))
                track[it, h, p, pl.ds(piece, MARK), :] = to_code(jnp.broadcast_to(code, (MARK, BLOCK)))

        loop(0, arcs, choose)

    def reduce_start(it, h):
        for d in PEERS:
            reduce_copy(it, h, d).start()

    def reduce_plane(it, h):
        def value(code):
            both = to_float(code)
            return both[:piece] * (level(both[piece : piece + 1]) * (1.0 / LEVELS))

        def add(d, acc):
            reduce_copy(it, h, d).wait_recv()
            return acc + value(partial[it, h, d])

        lane_sum[it, h] = lax.fori_loop(1, 16, add, value(track[it, h, q]))
        start(it, h, "xl")

    def weigh(it, h):
        own = pl.ds(pl.multiple_of(q * piece, piece), piece)
        arrived(it, h, "xl")
        full = lane_sum[it, h] + lane_got[it, h]
        seen = obs[own, pl.ds(h * BLOCK, BLOCK)].astype(F32)
        resid[it, h, core, own, :] = (weight_rows[own, :] * (full - seen)).astype(BF16)
        for d in PEERS:
            gather_copy(it, h, d).start()

    def place_resid(it, h, blk):
        def arc(a):
            month = arc_month[(hi * 2 + blk) * arcs + a]
            r = pl.multiple_of(a * rows, rows)
            w = resid[it, h, blk, pl.ds(r, rows), :].astype(F32)
            masked[blk, pl.ds(r, rows), pl.ds(0, BLOCK)] = jnp.where(month == pair_month, w, 0.0).astype(BF16)
            masked[blk, pl.ds(r, rows), pl.ds(BLOCK, BLOCK)] = jnp.where(month == g, w, 0.0).astype(BF16)

        loop(0, arcs, arc)

    def gradient_here(it, h):
        loop(1, 16, lambda d: gather_copy(it, h, d).wait_recv())
        start(it, h, "wm")
        place_resid(it, h, core)

        def part(c):
            r = pl.multiple_of(c * chunk, chunk)
            grad[h, pl.ds(r, chunk), :] = jnp.dot(
                turned[core, pl.ds(r, chunk), :], masked[core], preferred_element_type=F32
            )

        loop(0, CHUNKS, part)

    def gradient_mate(it, h, go):
        arrived(it, h, "wm")
        place_resid(it, h, 1 - core)
        for c in range(CHUNKS):
            part = pl.ds(c * chunk, chunk)
            grad[h, part, :] += jnp.dot(turned[1 - core, part, :], masked[1 - core], preferred_element_type=F32)

            encode(c, lambda r: grad[h, pl.ds(r, BLOCK), pl.ds(0, BLOCK)], grad_code.at[it, h])
            if go:
                start(it, h, f"gc{c}")

    def smooth(it, h):
        arrived(it, h, "hl", "hr")
        first = jnp.where(g == 0, 0.0, 1.0)
        last = jnp.where(g == 3, 0.0, 1.0)
        before, after = jnp.maximum(g - 1, 0), jnp.minimum(g + 1, 3)
        rims_in = to_float(rim[it, h, 0]), to_float(rim[it, h, 1])
        unit = level(rims_in[0][HALO + chunk_blocks - 1 : HALO + chunk_blocks]) * (1.0 / LEVELS)
        wide[it, h, pl.ds(0, HALO), :] = rims_in[0][:HALO] * unit
        unit = level(rims_in[1][:1]) * (1.0 / LEVELS)
        wide[it, h, pl.ds(HALO + cols, HALO), :] = rims_in[1][MARK:] * unit
        w = wide[it, h]
        high = w.astype(BF16)
        split[0] = high
        split[1] = (w - high.astype(F32)).astype(BF16)
        for c in range(CHUNKS):
            set_units(0, c, coded.at[it, h, before])
            set_units(1, c, coded.at[it, h, after])

            def body(b, r):
                high = split[0, pl.ds(r, 2 * BLOCK), :]
                window = jnp.concatenate([high, high, split[1, pl.ds(r, 2 * BLOCK), :]], axis=0)
                near = jnp.dot(stencil[c * chunk_blocks + b], window, preferred_element_type=F32)
                old = first * decode(0, coded.at[it, h, before], b, r)
                new = last * decode(1, coded.at[it, h, after], b, r)
                base[h, pl.ds(r, BLOCK), :] = (
                    wide[it, h, pl.ds(HALO + r, BLOCK), :] * keep_rows[pl.ds(r, BLOCK), :]
                    + near
                    + time_rows[pl.ds(r, BLOCK), :] * (old + new)
                )

            over_blocks(c, body)

    def store(h, c):
        part = pl.ds(c * chunk, chunk)
        return pltpu.make_async_copy(
            result.at[h, part], out_hbm.at[0, part, pl.ds(h * BLOCK, BLOCK)], store_sem.at[h, c]
        )

    def update(it, h, chunks=range(CHUNKS)):
        more = it < ITERS - 1
        for c in chunks:
            arrived(it, h, f"gc{c}")
            set_units(0, c, grad_code_in.at[it, h])

            def body(b, r):
                theirs = decode(0, grad_code_in.at[it, h], b, r)
                new = base[h, pl.ds(r, BLOCK), :] - step_rows[pl.ds(r, BLOCK), :] * (
                    grad[h, pl.ds(r, BLOCK), pl.ds(BLOCK, BLOCK)] + theirs
                )
                if it == ITERS - 1:
                    result[h, pl.ds(r, BLOCK), :] = new
                else:
                    wide[it + 1, h, pl.ds(HALO + r, BLOCK), :] = new

            over_blocks(c, body)
            if more:
                encode_state(it + 1, h, c)
                if h == 0 or c == 0:
                    start(it + 1, h, f"pc{c}")
            else:
                store(h, c).start()
        if more and CHUNKS - 1 in chunks:
            start(it + 1, h, *local)
            if h == 0:
                start(it + 1, h, *rims)

    turn = pltpu.make_async_remote_copy(
        src_ref=turned.at[core],
        dst_ref=turned.at[core],
        send_sem=turn_sem.at[0],
        recv_sem=turn_sem.at[1],
        device_id=mate,
        device_id_type=MESH,
    )

    def prepare():
        for load in loads[HALVES:]:
            load.wait()

        def arc(a):
            r = pl.multiple_of(a * rows, rows)
            turned[core, :, pl.ds(r, rows)] = panels[pl.ds(r, rows), :].T

        loop(0, arcs, arc)
        by_row = weights[...].astype(F32).T
        for a in range(arcs):
            weight_rows[a * rows : (a + 1) * rows, :] = jnp.broadcast_to(by_row[:, a : a + 1], (rows, BLOCK))

        count = neighbours.shape[0]
        here = s * cols + lax.broadcasted_iota(jnp.int32, (count, cols), 1)
        offset = neighbours[...] - here + HALO
        offset = jnp.where(offset < 0, offset + total, offset)
        offset = jnp.where(offset >= total, offset - total, offset)
        step = RELAX / diag[...]
        near = coef[...]
        own = jnp.sum(near, axis=0, keepdims=True)
        time = coupling[...].reshape(1, cols)
        table = jnp.concatenate(
            [offset.astype(F32), near * step, step, 1.0 - step * (own + 2.0 * time), step * time, jnp.zeros_like(step)],
            axis=0,
        )
        columns[...] = table.T

        def body(b):
            r = pl.multiple_of(b * BLOCK, BLOCK)
            part = columns[pl.ds(r, BLOCK), :]
            place = (
                lax.broadcasted_iota(jnp.int32, (BLOCK, 2 * BLOCK), 1)
                - lax.broadcasted_iota(jnp.int32, (BLOCK, 2 * BLOCK), 0)
            ).astype(F32)
            band = jnp.zeros((BLOCK, 2 * BLOCK), F32)
            for n in range(count):
                band = band + jnp.where(place == part[:, n : n + 1], part[:, count + n : count + n + 1], 0.0)
            high = band.astype(BF16)
            low = (band - high.astype(F32)).astype(BF16)
            stencil[b, :, pl.ds(0, 2 * BLOCK)] = high
            stencil[b, :, pl.ds(2 * BLOCK, 2 * BLOCK)] = low
            stencil[b, :, pl.ds(4 * BLOCK, 2 * BLOCK)] = high
            for k, where in enumerate((step_rows, keep_rows, time_rows)):
                where[pl.ds(r, BLOCK), :] = jnp.broadcast_to(
                    part[:, 2 * count + k : 2 * count + k + 1], (BLOCK, BLOCK)
                )

        loop(0, blocks, body)

    def settle(it, h):
        sent(it, h, *names)
        for d in PEERS:
            reduce_copy(it, h, d).wait_send()
            gather_copy(it, h, d).wait_send()

    for h in range(HALVES):
        loads[h].wait()
        for c in range(CHUNKS):
            encode_state(0, h, c)
        if h == 0:
            pl.semaphore_wait(barrier, 19)
            start(0, 0, *across)
        start(0, h, *local)
    prepare()
    chip_months(0, 0)
    sent(0, 0, *across)
    start(0, 0, *rims)
    start(0, 1, *across, *rims)
    far_arrive(0, 0)
    far_predict(0, 0)
    reduce_start(0, 0)
    turn.start()
    chip_months(0, 1)
    smooth(0, 0)
    far_arrive(0, 1)
    far_predict(0, 1)
    reduce_start(0, 1)
    reduce_plane(0, 0)
    weigh(0, 0)
    smooth(0, 1)
    turn.wait()
    reduce_plane(0, 1)
    gradient_here(0, 0)
    weigh(0, 1)
    gradient_mate(0, 0, True)
    gradient_here(0, 1)
    for it in range(1, ITERS):
        update(it - 1, 0, (0,))
        gradient_mate(it - 1, 1, False)
        update(it - 1, 0, (1,))
        start(it - 1, 1, "gc0", "gc1")
        chip_months(it, 0)
        far_arrive(it, 0)
        far_predict(it, 0)
        reduce_start(it, 0)
        smooth(it, 0)
        update(it - 1, 1)
        reduce_plane(it, 0)
        start(it, 1, "pc1", *rims)
        settle(it - 1, 0)
        chip_months(it, 1)
        weigh(it, 0)
        far_arrive(it, 1)
        far_predict(it, 1)
        reduce_start(it, 1)
        gradient_here(it, 0)
        gradient_mate(it, 0, False)
        reduce_plane(it, 1)
        start(it, 0, "gc0", "gc1")
        smooth(it, 1)
        settle(it - 1, 1)
        weigh(it, 1)
        gradient_here(it, 1)
    gradient_mate(ITERS - 1, 1, True)
    update(ITERS - 1, 0)
    settle(ITERS - 1, 0)
    update(ITERS - 1, 1)
    settle(ITERS - 1, 1)
    for h in range(HALVES):
        for c in range(CHUNKS):
            store(h, c).wait()


def on_device(panels, observations, data_weights, arc_month, fields, diag_scale, smooth_coef, neighbours, time_coupling):
    arcs, rows, cols = panels.shape
    samples = fields.shape[2]
    total = cols * lax.axis_size("mascon")
    every = arcs * rows
    piece = every // 16
    stages = (ITERS, HALVES)
    anywhere = pl.BlockSpec(memory_space=pl.ANY)
    return pl.pallas_call(
        functools.partial(kernel, (cols, arcs, rows, total)),
        out_shape=jax.ShapeDtypeStruct(fields.shape, F32),
        in_specs=[anywhere] * 9,
        out_specs=anywhere,
        scratch_shapes=[
            pltpu.SMEM(arc_month.shape, jnp.int32),
            pltpu.VMEM((every, cols), BF16),
            pltpu.VMEM((every, samples), BF16),
            pltpu.VMEM(data_weights.shape, BF16),
            pltpu.VMEM(diag_scale.shape, F32),
            pltpu.VMEM(smooth_coef.shape, F32),
            pltpu.VMEM(neighbours.shape, jnp.int32),
            pltpu.VMEM(time_coupling.shape, F32),
            pltpu.VMEM((HALVES, cols, BLOCK), F32),
            pltpu.VMEM((2, cols, every), BF16),
            pltpu.VMEM(stages + (cols + 2 * HALO, BLOCK), F32),
            pltpu.VMEM(stages + (4, cols + CHUNKS * MARK, BLOCK), I16),
            pltpu.VMEM(stages + (2, HALO + MARK, BLOCK), I16),
            pltpu.VMEM((MARK, BLOCK), F32),
            pltpu.VMEM((MARK, BLOCK), F32),
            pltpu.VMEM((2, MARK, BLOCK), F32),
            pltpu.VMEM((HALVES, cols, 4 * BLOCK), BF16),
            pltpu.VMEM((4, every, BLOCK), F32),
            pltpu.VMEM(stages + (16, piece + MARK, BLOCK), I16),
            pltpu.VMEM(stages + (16, piece + MARK, BLOCK), I16),
            pltpu.VMEM(stages + (piece, BLOCK), F32),
            pltpu.VMEM(stages + (piece, BLOCK), F32),
            pltpu.VMEM(stages + (2, every, BLOCK), BF16),
            pltpu.VMEM((2, every, 2 * BLOCK), BF16),
            pltpu.VMEM((HALVES, cols, 2 * BLOCK), F32),
            pltpu.VMEM(stages + (cols + CHUNKS * MARK, BLOCK), I16),
            pltpu.VMEM(stages + (cols + CHUNKS * MARK, BLOCK), I16),
            pltpu.VMEM((HALVES, cols, BLOCK), F32),
            pltpu.VMEM((every, BLOCK), F32),
            pltpu.VMEM((cols // BLOCK, BLOCK, 6 * BLOCK), BF16),
            pltpu.VMEM((cols, BLOCK), F32),
            pltpu.VMEM((cols, BLOCK), F32),
            pltpu.VMEM((cols, BLOCK), F32),
            pltpu.VMEM((cols, 16), F32),
            pltpu.VMEM((2, cols + 2 * HALO, BLOCK), BF16),
            pltpu.SemaphoreType.DMA((HALVES + 8,)),
            pltpu.SemaphoreType.DMA((HALVES, CHUNKS)),
            pltpu.SemaphoreType.DMA((ITERS * HALVES * 2, 16)),
            pltpu.SemaphoreType.DMA((ITERS * HALVES * 2, 16)),
            pltpu.SemaphoreType.DMA((ITERS * HALVES, 11)),
            pltpu.SemaphoreType.DMA((ITERS * HALVES, 11)),
            pltpu.SemaphoreType.DMA((2,)),
        ],
        compiler_params=pltpu.CompilerParams(
            collective_id=0, has_side_effects=True, vmem_limit_bytes=56 * 1024 * 1024
        ),
        cost_estimate=pl.CostEstimate(flops=6 * 10**9, bytes_accessed=8 * 10**6, transcendentals=0),
    )(
        arc_month,
        panels.reshape(every, cols),
        observations.reshape(every, samples),
        data_weights,
        fields,
        diag_scale,
        smooth_coef,
        neighbours,
        time_coupling,
    )


def solution(mesh):
    return jax.shard_map(
        on_device,
        mesh=mesh,
        in_specs=(
            P("month", None, "mascon"),
            P("month", None, None),
            P("month", None),
            P(),
            P("month", "mascon", None),
            P("month", "mascon"),
            P(None, "mascon"),
            P(None, "mascon"),
            P("mascon"),
        ),
        out_specs=P("month", "mascon", None),
        check_vma=False,
    )
```
